32 devices in a mesh: freq: 16 (over z, y, x), panel: 2 (over core).
Axes of the slice: x: 2, y: 2, z: 4, core: 2. Of those that a mesh axis runs over, the one named last changes fastest.
Arguments:
- shot_gathers: bfloat16 [64, 2048, 2048], P('freq', 'panel'), may hold values from -6 to 6
- aperture_blocks: int32 [32], replicated, may hold values from 8 to 16, as said below
- taper_index: int32 [32], replicated, may hold values from 0 to 3
Outputs:
- predicted: bfloat16 [64, 2048, 128], P('freq', 'panel')
The draws below stay inside these ranges and needn't reach their ends.
Inputs may be any that keep to these rules, and one draw needn't show every extreme that they name: `aperture_blocks`: aperture of each frequency in blocks of 128 surface points, counted from the first point; the largest value occurs in every draw.
All inputs are finite; a program needn't handle non-finite values.
Results may differ from the reference program's by a relative error of at most 0.0076.
Values may be sent and summed in bfloat16 or wider, within the bound.
A program may use at most 128 MiB of HBM per device.

```python
import math
import jax
import jax.numpy as jnp
from jax import lax

NR = 2048
SW = 128
BLOCK = 128
TAPER = 64
NF = 32
NT = 64


def draw_aperture_blocks(key, part):
    levels = NR // BLOCK
    drawn_level = jax.random.randint(key, (NF,), 0, levels, dtype=jnp.int32)
    counts = levels - drawn_level * drawn_level * (levels // 2) // ((levels - 1) * (levels - 1))
    top_place = jax.random.randint(jax.random.fold_in(key, 7), (), 0, NF, dtype=jnp.int32)
    return jnp.where(jnp.arange(NF, dtype=jnp.int32) == top_place, levels, counts).astype(jnp.int32)


def plant(result, own_key, least, largest):
    place = [jax.random.randint(jax.random.fold_in(own_key, axis), (), 0, length) for axis, length in enumerate(result.shape)]
    widest = result.shape.index(max(result.shape))
    beside = place[:widest] + [(place[widest] + 1) % result.shape[widest]] + place[widest + 1:]
    return result.at[tuple(place)].set(least).at[tuple(beside)].set(largest)


def level_of(stream_key, shape, pieces, low, largest):
    loudness, own = 1.0, jax.random.fold_in(stream_key, 6)
    for axis_at, parts in pieces:
        draws = jnp.exp(jax.random.uniform(jax.random.fold_in(own, axis_at), (parts,), jnp.float32, low / len(pieces), largest / len(pieces)))
        loudness = loudness * jnp.repeat(draws, shape[axis_at] // parts).reshape([-1 if axis == axis_at else 1 for axis in range(len(shape))])
    return loudness


def scatter_about(stream_key, shape, scale, most, cuts=(), held_as=jnp.bfloat16):
    result = scale * jax.random.normal(stream_key, shape, jnp.float32)
    if cuts:
        result = result * level_of(stream_key, shape, cuts, -0.22, 0.18)
    return jnp.clip(result, -most, most).astype(held_as)


def setup_inputs(seed: int = 0) -> dict:
    seeds = jax.random.split(jax.random.key(seed), 4)
    return {
        "shot_gathers": scatter_about(seeds[0], (NT, NR, NR), 1.0, 6.0, ((0, 16), (1, 2))),
        "aperture_blocks": draw_aperture_blocks(jax.random.fold_in(seeds[3], 71), 0),
        "taper_index": plant(jax.random.randint(seeds[2], (NF,), 0, 4), jax.random.fold_in(seeds[2], 1), 0, 3).astype(jnp.int32),
    }


def transform_tables(freq_total, time_total):
    bins = jnp.arange(freq_total, dtype=jnp.int32) + 1
    times = jnp.arange(time_total, dtype=jnp.int32)
    phase = bins[:, None] * times[None, :] % time_total
    angle = phase.astype(jnp.float32) * (2.0 * math.pi / time_total)
    scale = 1.0 / math.sqrt(time_total)
    forward = jnp.stack([jnp.cos(angle) * scale, -jnp.sin(angle) * scale], axis=1).astype(jnp.bfloat16)
    inverse = jnp.stack([jnp.cos(angle), -jnp.sin(angle)], axis=1).astype(jnp.bfloat16)
    return (forward, inverse)

def taper_weights(aperture, taper_level, surface_points):
    ends = aperture * BLOCK
    ramp = jnp.minimum(TAPER * (1 + taper_level), ends)
    begins = ends - ramp
    offset = (surface_points - begins + 1).astype(jnp.float32)
    wave = jnp.cos(0.5 * math.pi * offset / (ramp + 1).astype(jnp.float32))
    inside = jnp.where(surface_points < ends, wave * wave, jnp.zeros_like(wave))
    return jnp.where(surface_points < begins, jnp.ones_like(wave), inside)

def reference(shot_gathers, aperture_blocks, taper_index):
    forward, inverse = transform_tables(NF, NT)
    forward_wide = forward.astype(jnp.float32)
    inverse_wide = inverse.astype(jnp.float32)
    window = shot_gathers[:, :, :SW].astype(jnp.float32)
    window_spectra = jnp.einsum('fct,trs->fcrs', forward_wide, window).astype(jnp.bfloat16)
    surface_points = jnp.arange(NR, dtype=jnp.int32)
    weights = taper_weights(aperture_blocks[:, None], taper_index[:, None], surface_points[None, :])
    tapered = (weights[:, None, :, None] * window_spectra.astype(jnp.float32)).astype(jnp.bfloat16)
    tapered_wide = tapered.astype(jnp.float32)
    block_rows = NR // 16
    product_scale = -1.0 / math.sqrt(NR)
    output_scale = 1.0 / math.sqrt(NF)

    def one_block(block_index):
        rows = lax.dynamic_slice_in_dim(shot_gathers, (block_index * block_rows).astype(jnp.int32), block_rows, 1)
        spectra = jnp.einsum('fct,trk->fcrk', forward_wide, rows.astype(jnp.float32)).astype(jnp.bfloat16)
        spectra = lax.optimization_barrier(spectra).astype(jnp.float32)
        real_part = jnp.einsum('frk,fks->frs', spectra[:, 0], tapered_wide[:, 0]) - jnp.einsum('frk,fks->frs', spectra[:, 1], tapered_wide[:, 1])
        imag_part = jnp.einsum('frk,fks->frs', spectra[:, 0], tapered_wide[:, 1]) + jnp.einsum('frk,fks->frs', spectra[:, 1], tapered_wide[:, 0])
        multiples = (jnp.stack([real_part, imag_part], axis=1) * product_scale).astype(jnp.bfloat16)
        multiples = lax.optimization_barrier(multiples).astype(jnp.float32)
        traces = jnp.einsum('fct,fcrs->trs', inverse_wide, multiples) * output_scale
        return traces.astype(jnp.bfloat16)
    blocks = lax.map(one_block, jnp.arange(16, dtype=jnp.int32))
    return jnp.moveaxis(blocks, 0, 1).reshape(NT, NR, SW)
```

```python
import functools
import math

import jax
import jax.numpy as jnp
from jax import lax
from jax.experimental import pallas as pl
from jax.experimental.pallas import tpu as pltpu
from jax.sharding import PartitionSpec as P

SW = 128
BLOCK = 128
TAPER = 64
F_DEV = 2
RESPONSE_LIMIT = 2**26


def taper_weights(aperture, taper_level, surface_points):
    ends = aperture * BLOCK
    ramp = jnp.minimum(TAPER * (1 + taper_level), ends)
    begins = ends - ramp
    offset = (surface_points - begins + 1).astype(jnp.float32)
    wave = jnp.cos(0.5 * math.pi * offset / (ramp + 1).astype(jnp.float32))
    inside = jnp.where(surface_points < ends, wave * wave, jnp.zeros_like(wave))
    return jnp.where(surface_points < begins, jnp.ones_like(wave), inside)


def convolve_kernel(j_ref, d_ref, cur_ref, prev_ref, out_ref, pairs):
    steps, rows, points = d_ref.shape

    def slab(m):
        part = cur_ref[:, m] if m >= 0 else prev_ref[:, steps + m]
        return part.reshape(points, SW)

    for m in range(1 - steps, steps - 1):
        at = m + steps - 1
        pairs[at, :, :SW] = slab(m)
        pairs[at, :, SW:] = slab(m + 1)
    tile = 256

    @pl.loop(0, rows // tile)
    def _(r):
        here = pl.ds(pl.multiple_of(r * tile, tile), tile)
        for q in range(0, steps, 2):
            total = None
            for i in range(steps):
                term = jnp.dot(
                    d_ref[i, here, :], pairs[q - i + steps - 1], preferred_element_type=jnp.float32
                )
                total = term if total is None else total + term
            out_ref[q, here, :] = total[:, :SW].astype(jnp.bfloat16)
            out_ref[q + 1, here, :] = total[:, SW:].astype(jnp.bfloat16)


def convolve(index, data, response):
    steps, rows, points = data.shape
    groups, times, each, _ = response.shape
    count = times // steps
    return pl.pallas_call(
        convolve_kernel,
        grid_spec=pltpu.PrefetchScalarGridSpec(
            num_scalar_prefetch=1,
            grid=(count,),
            in_specs=[
                pl.BlockSpec((steps, rows, points), lambda b, j: (0, 0, 0), pipeline_mode=pl.Buffered(1)),
                pl.BlockSpec((groups, steps, each, SW), lambda b, j: (0, b, 0, 0)),
                pl.BlockSpec(
                    (groups, steps, each, SW), lambda b, j: (0, lax.rem(b + count - 1, count), 0, 0)
                ),
            ],
            out_specs=pl.BlockSpec(
                (steps, rows, SW), lambda b, j: (lax.rem(b + j[0], count), 0, 0)
            ),
            scratch_shapes=[pltpu.VMEM((2 * steps - 2, points, 2 * SW), jnp.bfloat16)],
        ),
        out_shape=jax.ShapeDtypeStruct((times, rows, SW), jnp.bfloat16),
        compiler_params=pltpu.CompilerParams(vmem_limit_bytes=56 * 2**20),
        cost_estimate=pl.CostEstimate(
            flops=2 * steps * rows * points * SW * times,
            bytes_accessed=2 * (steps * rows * points + 2 * times * points * SW + times * rows * SW),
            transcendentals=0,
        ),
    )(index, data, response, response)


def angles(freq_total, time_total):
    bins = jnp.arange(freq_total, dtype=jnp.int32) + 1
    times = jnp.arange(time_total, dtype=jnp.int32)
    phase = bins[:, None] * times[None, :] % time_total
    return phase.astype(jnp.float32) * (2.0 * math.pi / time_total)


def window_response(window, aperture_blocks, taper_index, points, points_total):
    time_total, count, _ = window.shape
    freq_total = aperture_blocks.shape[0]
    angle = angles(freq_total, time_total)
    forward = jnp.stack([jnp.cos(angle), -jnp.sin(angle)], axis=1) * (1.0 / math.sqrt(time_total))
    spectra = jnp.einsum(
        "fct,tks->fcks", forward.astype(jnp.bfloat16), window, preferred_element_type=jnp.float32
    ).astype(jnp.bfloat16)
    weights = taper_weights(aperture_blocks[:, None], taper_index[:, None], points[None, :])
    tapered = (weights[:, None, :, None] * spectra.astype(jnp.float32)).astype(jnp.bfloat16)
    scale = -1.0 / math.sqrt(time_total * points_total * freq_total)
    back = jnp.stack([jnp.cos(angle), -jnp.sin(angle)], axis=1) * scale
    return jnp.einsum(
        "fct,fcks->tks", back, tapered.astype(jnp.float32), precision=lax.Precision.HIGHEST
    ).astype(jnp.bfloat16)


def body(shot_gathers, aperture_blocks, taper_index):
    steps, rows, points_total = shot_gathers.shape
    owners = lax.axis_size("freq")
    if 2 * steps * owners * points_total * SW > RESPONSE_LIMIT:
        return frequency_body(shot_gathers, aperture_blocks, taper_index)
    index = lax.axis_index("freq").astype(jnp.int32)
    each = rows // owners
    window = lax.all_to_all(
        shot_gathers[:, :, :SW], "freq", split_axis=1, concat_axis=0, tiled=True
    )
    points = lax.axis_index("panel") * rows + index * each + jnp.arange(each, dtype=jnp.int32)
    response = window_response(window, aperture_blocks, taper_index, points, points_total)
    response = lax.all_gather(response, ("panel", "freq"), axis=0, tiled=False)
    partial = convolve(index[None], shot_gathers, response)
    return lax.psum_scatter(partial, "freq", scatter_dimension=0, tiled=True)


def transform_tables(freq_total, time_total):
    bins = jnp.arange(freq_total, dtype=jnp.int32) + 1
    times = jnp.arange(time_total, dtype=jnp.int32)
    phase = bins[:, None] * times[None, :] % time_total
    angle = phase.astype(jnp.float32) * (2.0 * math.pi / time_total)
    scale = 1.0 / math.sqrt(time_total)
    forward = jnp.stack([jnp.cos(angle) * scale, -jnp.sin(angle) * scale], axis=1).astype(
        jnp.bfloat16
    )
    inverse = jnp.stack([jnp.cos(angle), -jnp.sin(angle)], axis=1).astype(jnp.bfloat16)
    return (forward, inverse)


def frequency_body(shot_gathers, aperture_blocks, taper_index):
    time_local, rows_local, points_total = shot_gathers.shape
    owners = lax.axis_size("freq")
    slot_count = 2 * F_DEV
    time_total = time_local * owners
    freq_total = F_DEV * owners
    owner_index = lax.axis_index("freq")
    panel_index = lax.axis_index("panel")
    owner_range = jnp.arange(owners, dtype=jnp.int32)
    freq_range = jnp.arange(freq_total, dtype=jnp.int32)
    assignment = freq_range.reshape(owners, F_DEV)
    forward, inverse = transform_tables(freq_total, time_total)
    selector = (assignment.reshape(-1)[:, None] == freq_range[None, :]).astype(jnp.bfloat16)
    picked_forward = jnp.dot(
        selector, forward.reshape(freq_total, 2 * time_total), preferred_element_type=jnp.float32
    ).astype(jnp.bfloat16)
    forward_rows = (
        picked_forward.reshape(owners, F_DEV, 2, time_total)
        .transpose(1, 2, 0, 3)
        .reshape(slot_count, owners, time_total)
    )
    picked_inverse = jnp.dot(
        selector, inverse.reshape(freq_total, 2 * time_total), preferred_element_type=jnp.float32
    ).astype(jnp.bfloat16)
    inverse_rows = picked_inverse.reshape(owners * slot_count, owners, time_local)
    trace_width = rows_local * points_total // owners
    outgoing_time = shot_gathers.reshape(time_local, owners, trace_width)
    series = lax.all_to_all(outgoing_time, "freq", split_axis=1, concat_axis=0, tiled=True)[:, 0, :]
    spectra = jnp.einsum(
        "qot,tw->qow", forward_rows, series, preferred_element_type=jnp.float32
    ).astype(jnp.bfloat16)
    own_spectra = lax.all_to_all(spectra, "freq", split_axis=1, concat_axis=1, tiled=True)
    own_spectra = own_spectra.reshape(F_DEV, 2, rows_local, points_total)
    mine = owner_range[:, None] == owner_index
    my_freqs = jnp.sum(jnp.where(mine, assignment, jnp.zeros_like(assignment)), axis=0)
    matches = my_freqs[:, None] == freq_range[None, :]
    my_aperture = jnp.sum(jnp.where(matches, aperture_blocks[None, :], 0), axis=1)
    my_taper = jnp.sum(jnp.where(matches, taper_index[None, :], 0), axis=1)
    local_points = panel_index * rows_local + jnp.arange(rows_local, dtype=jnp.int32)
    weights = taper_weights(my_aperture[:, None], my_taper[:, None], local_points[None, :])
    tapered = (weights[:, None, :, None] * own_spectra[:, :, :, :SW].astype(jnp.float32)).astype(
        jnp.bfloat16
    )
    piece = lax.all_gather(tapered, "panel", axis=2, tiled=True)
    updated_list = []
    for slot_index in range(F_DEV):
        left_block = own_spectra[slot_index]
        stacked_left = jnp.concatenate([left_block[0], left_block[1]], axis=1)
        real_side = jnp.concatenate([piece[slot_index, 0], -piece[slot_index, 1]], axis=0)
        imag_side = jnp.concatenate([piece[slot_index, 1], piece[slot_index, 0]], axis=0)
        stacked_right = jnp.stack([real_side, imag_side], axis=0)
        updated = jnp.einsum(
            "rk,cks->crs", stacked_left, stacked_right, preferred_element_type=jnp.float32
        )
        updated_list.append(updated)
    summed = jnp.stack(updated_list, axis=0)
    multiples = (summed * (-1.0 / math.sqrt(points_total))).astype(jnp.bfloat16)
    output_width = rows_local * SW // owners
    outgoing_freq = multiples.reshape(slot_count, owners, output_width)
    output_scale = 1.0 / math.sqrt(freq_total)
    values = lax.all_to_all(outgoing_freq, "freq", split_axis=1, concat_axis=0, tiled=True)[:, 0, :]
    traces = (
        jnp.einsum("qgt,qw->tgw", inverse_rows, values, preferred_element_type=jnp.float32)
        * output_scale
    )
    result = lax.all_to_all(
        traces.astype(jnp.bfloat16), "freq", split_axis=1, concat_axis=1, tiled=True
    )
    return result.reshape(time_local, rows_local, SW)


def solution(mesh):
    return jax.shard_map(
        body,
        mesh=mesh,
        in_specs=(P("freq", "panel", None), P(), P()),
        out_specs=P("freq", "panel", None),
        check_vma=False,
    )
```

```python
import functools
import math

import jax
import jax.numpy as jnp
from jax import lax
from jax.experimental import pallas as pl
from jax.experimental.pallas import tpu as pltpu
from jax.sharding import PartitionSpec as P

SW = 128
BLOCK = 128
TAPER = 64
F_DEV = 2
RESPONSE_LIMIT = 2**26


def taper_weights(aperture, taper_level, surface_points):
    ends = aperture * BLOCK
    ramp = jnp.minimum(TAPER * (1 + taper_level), ends)
    begins = ends - ramp
    offset = (surface_points - begins + 1).astype(jnp.float32)
    wave = jnp.cos(0.5 * math.pi * offset / (ramp + 1).astype(jnp.float32))
    inside = jnp.where(surface_points < ends, wave * wave, jnp.zeros_like(wave))
    return jnp.where(surface_points < begins, jnp.ones_like(wave), inside)


def ring_place(index, levels):
    z, y, x = index // 4, index // 2 % 2, index % 2
    column = 2 * y + x + y - 2 * x * y
    return column * levels + z + column % 2 * (levels - 1 - 2 * z)


def ring_index(place, levels):
    column, along = place // levels, place % levels
    z = along + column % 2 * (levels - 1 - 2 * along)
    y = column // 2
    return 4 * z + 2 * y + (column + y) % 2


def convolve_kernel(
    owners, d_hbm, h_hbm, out_ref, data, pairs, total_ref, send, from_left, from_right,
    data_sem, pair_sem, send_sem, left_sem, right_sem,
):
    steps, rows, points = d_hbm.shape
    times = steps * owners
    groups, each = h_hbm.shape[0], h_hbm.shape[2]
    levels = owners // 4
    half = owners // 2
    tile = 256
    me = lax.axis_index("freq")
    place = ring_place(me, levels)
    right = ring_index((place + 1) % owners, levels)
    left = ring_index((place + owners - 1) % owners, levels)

    barrier = pltpu.get_barrier_semaphore()
    for neighbour in (left, right):
        pl.semaphore_signal(
            barrier, inc=1, device_id={"freq": neighbour}, device_id_type=pl.DeviceIdType.MESH
        )

    def pair_copies(buffer, base):
        copies = []
        for at in range(2 * steps - 2):
            for side in range(2):
                tau = (base + at + side + times + 1 - steps) % times
                copies.append(
                    pltpu.make_async_copy(
                        h_hbm.at[:, tau],
                        pairs.at[buffer, at, :, :, pl.ds(side * SW, SW)],
                        pair_sem.at[buffer, 2 * at + side],
                    )
                )
        return copies

    def fetch(buffer, distance):
        owner = ring_index((place + distance + owners) % owners, levels)
        for copy in pair_copies(buffer, steps * ((owner - me + owners) % owners)):
            copy.start()

    def compute(buffer):
        for copy in pair_copies(buffer, 0):
            copy.wait()

        @pl.loop(0, rows // tile)
        def _(r):
            here = pl.ds(pl.multiple_of(r * tile, tile), tile)
            for q in range(0, steps, 2):
                total = None
                for i in range(steps):
                    term = jnp.dot(
                        data[i, here, :],
                        pairs[buffer, q - i + steps - 1].reshape(points, 2 * SW),
                        preferred_element_type=jnp.float32,
                    )
                    total = term if total is None else total + term
                total_ref[q, here, :] = total[:, :SW]
                total_ref[q + 1, here, :] = total[:, SW:]

    def store(target, terms):
        @pl.loop(0, rows // tile)
        def _(r):
            here = pl.ds(pl.multiple_of(r * tile, tile), tile)
            for q in range(steps):
                value = total_ref[q, here, :]
                for term in terms:
                    value = value + term[q, here, :].astype(jnp.float32)
                target[q, here, :] = value.astype(jnp.bfloat16)

    def sending(way, distance):
        landing, sem, to = ((from_left, left_sem, right), (from_right, right_sem, left))[way]
        return pltpu.make_async_remote_copy(
            src_ref=send.at[way, distance % 2],
            dst_ref=landing.at[distance - 1],
            send_sem=send_sem.at[way, distance % 2],
            recv_sem=sem.at[distance - 1],
            device_id={"freq": to},
            device_id_type=pl.DeviceIdType.MESH,
        )

    load = pltpu.make_async_copy(d_hbm, data, data_sem)
    load.start()
    fetch(0, half)
    fetch(1, 1 - half)
    load.wait()

    compute(0)
    fetch(0, half - 1)
    store(send.at[0, half % 2], [])
    pl.semaphore_wait(barrier, 2)
    sending(0, half).start()

    @pl.loop(0, half - 1)
    def _(n):
        distance = half - 1 - n
        compute(1)
        fetch(1, 1 - distance)

        @pl.when(n >= 2)
        def _():
            sending(1, distance + 2).wait_send()

        @pl.when(n >= 1)
        def _():
            sending(1, distance + 1).wait_recv()
            store(send.at[1, distance % 2], [from_right.at[distance]])

        @pl.when(n == 0)
        def _():
            store(send.at[1, distance % 2], [])

        sending(1, distance).start()
        compute(0)

        @pl.when(distance > 1)
        def _():
            fetch(0, distance - 1)

        @pl.when(n >= 1)
        def _():
            sending(0, distance + 2).wait_send()

        sending(0, distance + 1).wait_recv()
        store(send.at[0, distance % 2], [from_left.at[distance]])
        sending(0, distance).start()

    compute(1)
    sending(0, 1).wait_recv()
    sending(1, 1).wait_recv()
    store(out_ref, [from_left.at[0], from_right.at[0]])
    for way in range(2):
        for distance in (2, 1):
            sending(way, distance).wait_send()


def convolve(data, response, owners):
    steps, rows, points = data.shape
    groups, times, each, _ = response.shape
    half = owners // 2
    block = (steps, rows, SW)
    return pl.pallas_call(
        functools.partial(convolve_kernel, owners),
        in_specs=[pl.BlockSpec(memory_space=pl.ANY)] * 2,
        out_specs=pl.BlockSpec(memory_space=pltpu.VMEM),
        out_shape=jax.ShapeDtypeStruct(block, jnp.bfloat16),
        scratch_shapes=[
            pltpu.VMEM(data.shape, jnp.bfloat16),
            pltpu.VMEM((2, 2 * steps - 2, groups, each, 2 * SW), jnp.bfloat16),
            pltpu.VMEM(block, jnp.float32),
            pltpu.VMEM((2, 2) + block, jnp.bfloat16),
            pltpu.VMEM((half,) + block, jnp.bfloat16),
            pltpu.VMEM((half - 1,) + block, jnp.bfloat16),
            pltpu.SemaphoreType.DMA,
            pltpu.SemaphoreType.DMA((2, 4 * steps - 4)),
            pltpu.SemaphoreType.DMA((2, 2)),
            pltpu.SemaphoreType.DMA((half,)),
            pltpu.SemaphoreType.DMA((half - 1,)),
        ],
        compiler_params=pltpu.CompilerParams(
            vmem_limit_bytes=58 * 2**20, collective_id=0, has_side_effects=True
        ),
        cost_estimate=pl.CostEstimate(
            flops=2 * steps * rows * points * SW * times,
            bytes_accessed=2 * (steps * rows * points + 3 * times * points * SW),
            transcendentals=0,
        ),
    )(data, response)


def angles(freq_total, time_total):
    bins = jnp.arange(freq_total, dtype=jnp.int32) + 1
    times = jnp.arange(time_total, dtype=jnp.int32)
    phase = bins[:, None] * times[None, :] % time_total
    return phase.astype(jnp.float32) * (2.0 * math.pi / time_total)


def window_response(window, aperture_blocks, taper_index, points, points_total):
    time_total, count, _ = window.shape
    freq_total = aperture_blocks.shape[0]
    angle = angles(freq_total, time_total)
    forward = jnp.stack([jnp.cos(angle), -jnp.sin(angle)], axis=1) * (1.0 / math.sqrt(time_total))
    spectra = jnp.einsum(
        "fct,tks->fcks", forward.astype(jnp.bfloat16), window, preferred_element_type=jnp.float32
    ).astype(jnp.bfloat16)
    weights = taper_weights(aperture_blocks[:, None], taper_index[:, None], points[None, :])
    tapered = (weights[:, None, :, None] * spectra.astype(jnp.float32)).astype(jnp.bfloat16)
    scale = -1.0 / math.sqrt(time_total * points_total * freq_total)
    back = jnp.stack([jnp.cos(angle), -jnp.sin(angle)], axis=1) * scale
    return jnp.einsum(
        "fct,fcks->tks", back, tapered.astype(jnp.float32), precision=lax.Precision.HIGHEST
    ).astype(jnp.bfloat16)


def body(shot_gathers, aperture_blocks, taper_index):
    steps, rows, points_total = shot_gathers.shape
    owners = lax.axis_size("freq")
    if 2 * steps * owners * points_total * SW > RESPONSE_LIMIT:
        return frequency_body(shot_gathers, aperture_blocks, taper_index)
    index = lax.axis_index("freq")
    each = rows // owners
    window = lax.all_to_all(
        shot_gathers[:, :, :SW], "freq", split_axis=1, concat_axis=0, tiled=True
    )
    points = lax.axis_index("panel") * rows + index * each + jnp.arange(each, dtype=jnp.int32)
    response = window_response(window, aperture_blocks, taper_index, points, points_total)
    response = lax.all_gather(
        response.reshape(-1, SW), ("panel", "freq"), axis=0, tiled=True
    ).reshape(-1, steps * owners, each, SW)
    return convolve(shot_gathers, response, owners)


def transform_tables(freq_total, time_total):
    bins = jnp.arange(freq_total, dtype=jnp.int32) + 1
    times = jnp.arange(time_total, dtype=jnp.int32)
    phase = bins[:, None] * times[None, :] % time_total
    angle = phase.astype(jnp.float32) * (2.0 * math.pi / time_total)
    scale = 1.0 / math.sqrt(time_total)
    forward = jnp.stack([jnp.cos(angle) * scale, -jnp.sin(angle) * scale], axis=1).astype(
        jnp.bfloat16
    )
    inverse = jnp.stack([jnp.cos(angle), -jnp.sin(angle)], axis=1).astype(jnp.bfloat16)
    return (forward, inverse)


def frequency_body(shot_gathers, aperture_blocks, taper_index):
    time_local, rows_local, points_total = shot_gathers.shape
    owners = lax.axis_size("freq")
    slot_count = 2 * F_DEV
    time_total = time_local * owners
    freq_total = F_DEV * owners
    owner_index = lax.axis_index("freq")
    panel_index = lax.axis_index("panel")
    owner_range = jnp.arange(owners, dtype=jnp.int32)
    freq_range = jnp.arange(freq_total, dtype=jnp.int32)
    assignment = freq_range.reshape(owners, F_DEV)
    forward, inverse = transform_tables(freq_total, time_total)
    selector = (assignment.reshape(-1)[:, None] == freq_range[None, :]).astype(jnp.bfloat16)
    picked_forward = jnp.dot(
        selector, forward.reshape(freq_total, 2 * time_total), preferred_element_type=jnp.float32
    ).astype(jnp.bfloat16)
    forward_rows = (
        picked_forward.reshape(owners, F_DEV, 2, time_total)
        .transpose(1, 2, 0, 3)
        .reshape(slot_count, owners, time_total)
    )
    picked_inverse = jnp.dot(
        selector, inverse.reshape(freq_total, 2 * time_total), preferred_element_type=jnp.float32
    ).astype(jnp.bfloat16)
    inverse_rows = picked_inverse.reshape(owners * slot_count, owners, time_local)
    trace_width = rows_local * points_total // owners
    outgoing_time = shot_gathers.reshape(time_local, owners, trace_width)
    series = lax.all_to_all(outgoing_time, "freq", split_axis=1, concat_axis=0, tiled=True)[:, 0, :]
    spectra = jnp.einsum(
        "qot,tw->qow", forward_rows, series, preferred_element_type=jnp.float32
    ).astype(jnp.bfloat16)
    own_spectra = lax.all_to_all(spectra, "freq", split_axis=1, concat_axis=1, tiled=True)
    own_spectra = own_spectra.reshape(F_DEV, 2, rows_local, points_total)
    mine = owner_range[:, None] == owner_index
    my_freqs = jnp.sum(jnp.where(mine, assignment, jnp.zeros_like(assignment)), axis=0)
    matches = my_freqs[:, None] == freq_range[None, :]
    my_aperture = jnp.sum(jnp.where(matches, aperture_blocks[None, :], 0), axis=1)
    my_taper = jnp.sum(jnp.where(matches, taper_index[None, :], 0), axis=1)
    local_points = panel_index * rows_local + jnp.arange(rows_local, dtype=jnp.int32)
    weights = taper_weights(my_aperture[:, None], my_taper[:, None], local_points[None, :])
    tapered = (weights[:, None, :, None] * own_spectra[:, :, :, :SW].astype(jnp.float32)).astype(
        jnp.bfloat16
    )
    piece = lax.all_gather(tapered, "panel", axis=2, tiled=True)
    updated_list = []
    for slot_index in range(F_DEV):
        left_block = own_spectra[slot_index]
        stacked_left = jnp.concatenate([left_block[0], left_block[1]], axis=1)
        real_side = jnp.concatenate([piece[slot_index, 0], -piece[slot_index, 1]], axis=0)
        imag_side = jnp.concatenate([piece[slot_index, 1], piece[slot_index, 0]], axis=0)
        stacked_right = jnp.stack([real_side, imag_side], axis=0)
        updated = jnp.einsum(
            "rk,cks->crs", stacked_left, stacked_right, preferred_element_type=jnp.float32
        )
        updated_list.append(updated)
    summed = jnp.stack(updated_list, axis=0)
    multiples = (summed * (-1.0 / math.sqrt(points_total))).astype(jnp.bfloat16)
    output_width = rows_local * SW // owners
    outgoing_freq = multiples.reshape(slot_count, owners, output_width)
    output_scale = 1.0 / math.sqrt(freq_total)
    values = lax.all_to_all(outgoing_freq, "freq", split_axis=1, concat_axis=0, tiled=True)[:, 0, :]
    traces = (
        jnp.einsum("qgt,qw->tgw", inverse_rows, values, preferred_element_type=jnp.float32)
        * output_scale
    )
    result = lax.all_to_all(
        traces.astype(jnp.bfloat16), "freq", split_axis=1, concat_axis=1, tiled=True
    )
    return result.reshape(time_local, rows_local, SW)


def solution(mesh):
    return jax.shard_map(
        body,
        mesh=mesh,
        in_specs=(P("freq", "panel", None), P(), P()),
        out_specs=P("freq", "panel", None),
        check_vma=False,
    )
```

```python
import functools
import math

import jax
import jax.numpy as jnp
from jax import lax
from jax.experimental import pallas as pl
from jax.experimental.pallas import tpu as pltpu
from jax.sharding import PartitionSpec as P

SW = 128
BLOCK = 128
TAPER = 64
F_DEV = 2
RESPONSE_LIMIT = 2**26


def taper_weights(aperture, taper_level, surface_points):
    ends = aperture * BLOCK
    ramp = jnp.minimum(TAPER * (1 + taper_level), ends)
    begins = ends - ramp
    offset = (surface_points - begins + 1).astype(jnp.float32)
    wave = jnp.cos(0.5 * math.pi * offset / (ramp + 1).astype(jnp.float32))
    inside = jnp.where(surface_points < ends, wave * wave, jnp.zeros_like(wave))
    return jnp.where(surface_points < begins, jnp.ones_like(wave), inside)


def ring_place(index, levels):
    z, y, x = index // 4, index // 2 % 2, index % 2
    column = 2 * y + x + y - 2 * x * y
    return column * levels + z + column % 2 * (levels - 1 - 2 * z)


def ring_index(place, levels):
    column, along = place // levels, place % levels
    z = along + column % 2 * (levels - 1 - 2 * along)
    y = column // 2
    return 4 * z + 2 * y + (column + y) % 2


def convolve_kernel(
    owners, d_hbm, h_hbm, out_ref, data, pairs, total_ref, send, from_left, from_right,
    data_sem, pair_sem, send_sem, left_sem, right_sem,
):
    steps, rows, points = d_hbm.shape
    times = steps * owners
    groups, each = h_hbm.shape[0], h_hbm.shape[2]
    levels = owners // 4
    half = owners // 2
    tile = 256
    me = lax.axis_index("freq")
    place = ring_place(me, levels)
    right = ring_index((place + 1) % owners, levels)
    left = ring_index((place + owners - 1) % owners, levels)

    barrier = pltpu.get_barrier_semaphore()
    for neighbour in (left, right):
        pl.semaphore_signal(
            barrier, inc=1, device_id={"freq": neighbour}, device_id_type=pl.DeviceIdType.MESH
        )

    def pair_copies(buffer, base):
        copies = []
        for at in range(2 * steps - 2):
            for side in range(2):
                tau = (base + at + side + times + 1 - steps) % times
                copies.append(
                    pltpu.make_async_copy(
                        h_hbm.at[:, tau],
                        pairs.at[buffer, at, :, :, pl.ds(side * SW, SW)],
                        pair_sem.at[buffer, 2 * at + side],
                    )
                )
        return copies

    def fetch(buffer, distance):
        owner = ring_index((place + distance + owners) % owners, levels)
        for copy in pair_copies(buffer, steps * ((owner - me + owners) % owners)):
            copy.start()

    def compute(buffer):
        for copy in pair_copies(buffer, 0):
            copy.wait()

        @pl.loop(0, rows // tile)
        def _(r):
            here = pl.ds(pl.multiple_of(r * tile, tile), tile)
            for q in range(0, steps, 2):
                total = None
                for i in range(steps):
                    term = jnp.dot(
                        data[i, here, :],
                        pairs[buffer, q - i + steps - 1].reshape(points, 2 * SW),
                        preferred_element_type=jnp.float32,
                    )
                    total = term if total is None else total + term
                total_ref[q, here, :] = total[:, :SW]
                total_ref[q + 1, here, :] = total[:, SW:]

    def store(target, terms):
        @pl.loop(0, rows // tile)
        def _(r):
            here = pl.ds(pl.multiple_of(r * tile, tile), tile)
            for q in range(steps):
                value = total_ref[q, here, :]
                for term in terms:
                    value = value + term[q, here, :].astype(jnp.float32)
                target[q, here, :] = value.astype(jnp.bfloat16)

    def sending(way, distance):
        landing, sem, to = ((from_left, left_sem, right), (from_right, right_sem, left))[way]
        return pltpu.make_async_remote_copy(
            src_ref=send.at[way, distance % 2],
            dst_ref=landing.at[distance - 1],
            send_sem=send_sem.at[way, distance % 2],
            recv_sem=sem.at[distance - 1],
            device_id={"freq": to},
            device_id_type=pl.DeviceIdType.MESH,
        )

    load = pltpu.make_async_copy(d_hbm, data, data_sem)
    load.start()
    fetch(0, half)
    fetch(1, 1 - half)
    load.wait()

    compute(0)
    fetch(0, half - 1)
    store(send.at[0, half % 2], [])
    pl.semaphore_wait(barrier, 2)
    sending(0, half).start()

    @pl.loop(0, half - 1)
    def _(n):
        distance = half - 1 - n
        compute(1)
        fetch(1, 1 - distance)

        @pl.when(n >= 2)
        def _():
            sending(1, distance + 2).wait_send()

        @pl.when(n >= 1)
        def _():
            sending(1, distance + 1).wait_recv()
            store(send.at[1, distance % 2], [from_right.at[distance]])

        @pl.when(n == 0)
        def _():
            store(send.at[1, distance % 2], [])

        sending(1, distance).start()
        compute(0)

        @pl.when(distance > 1)
        def _():
            fetch(0, distance - 1)

        @pl.when(n >= 1)
        def _():
            sending(0, distance + 2).wait_send()

        sending(0, distance + 1).wait_recv()
        store(send.at[0, distance % 2], [from_left.at[distance]])
        sending(0, distance).start()

    compute(1)
    sending(0, 1).wait_recv()
    sending(1, 1).wait_recv()
    store(out_ref, [from_left.at[0], from_right.at[0]])
    for way in range(2):
        for distance in (2, 1):
            sending(way, distance).wait_send()


def convolve(data, response, owners):
    steps, rows, points = data.shape
    groups, times, each, _ = response.shape
    half = owners // 2
    block = (steps, rows, SW)
    return pl.pallas_call(
        functools.partial(convolve_kernel, owners),
        in_specs=[pl.BlockSpec(memory_space=pl.ANY)] * 2,
        out_specs=pl.BlockSpec(memory_space=pltpu.VMEM),
        out_shape=jax.ShapeDtypeStruct(block, jnp.bfloat16),
        scratch_shapes=[
            pltpu.VMEM(data.shape, jnp.bfloat16),
            pltpu.VMEM((2, 2 * steps - 2, groups, each, 2 * SW), jnp.bfloat16),
            pltpu.VMEM(block, jnp.float32),
            pltpu.VMEM((2, 2) + block, jnp.bfloat16),
            pltpu.VMEM((half,) + block, jnp.bfloat16),
            pltpu.VMEM((half - 1,) + block, jnp.bfloat16),
            pltpu.SemaphoreType.DMA,
            pltpu.SemaphoreType.DMA((2, 4 * steps - 4)),
            pltpu.SemaphoreType.DMA((2, 2)),
            pltpu.SemaphoreType.DMA((half,)),
            pltpu.SemaphoreType.DMA((half - 1,)),
        ],
        compiler_params=pltpu.CompilerParams(
            vmem_limit_bytes=58 * 2**20, collective_id=0, has_side_effects=True
        ),
        cost_estimate=pl.CostEstimate(
            flops=2 * steps * rows * points * SW * times,
            bytes_accessed=2 * (steps * rows * points + 3 * times * points * SW),
            transcendentals=0,
        ),
    )(data, response)


def angles(freq_total, time_total):
    bins = jnp.arange(freq_total, dtype=jnp.int32) + 1
    times = jnp.arange(time_total, dtype=jnp.int32)
    phase = bins[:, None] * times[None, :] % time_total
    return phase.astype(jnp.float32) * (2.0 * math.pi / time_total)


def window_response(window, aperture_blocks, taper_index, points, points_total):
    time_total, count, _ = window.shape
    freq_total = aperture_blocks.shape[0]
    angle = angles(freq_total, time_total)
    forward = jnp.stack([jnp.cos(angle), -jnp.sin(angle)], axis=1) * (1.0 / math.sqrt(time_total))
    spectra = jnp.einsum(
        "fct,tks->fcks", forward.astype(jnp.bfloat16), window, preferred_element_type=jnp.float32
    ).astype(jnp.bfloat16)
    weights = taper_weights(aperture_blocks[:, None], taper_index[:, None], points[None, :])
    tapered = (weights[:, None, :, None] * spectra.astype(jnp.float32)).astype(jnp.bfloat16)
    scale = -1.0 / math.sqrt(time_total * points_total * freq_total)
    back = jnp.stack([jnp.cos(angle), -jnp.sin(angle)], axis=1) * scale
    return jnp.einsum(
        "fct,fcks->tks", back, tapered.astype(jnp.float32), precision=lax.Precision.HIGHEST
    ).astype(jnp.bfloat16)


def body(shot_gathers, aperture_blocks, taper_index):
    steps, rows, points_total = shot_gathers.shape
    owners = lax.axis_size("freq")
    if 2 * steps * owners * points_total * SW > RESPONSE_LIMIT:
        return frequency_body(shot_gathers, aperture_blocks, taper_index)
    index = lax.axis_index("freq")
    each = rows // owners
    window = lax.all_to_all(
        shot_gathers[:, :, :SW], "freq", split_axis=1, concat_axis=0, tiled=True
    )
    points = lax.axis_index("panel") * rows + index * each + jnp.arange(each, dtype=jnp.int32)
    response = window_response(window, aperture_blocks, taper_index, points, points_total)
    response = lax.all_gather(response.reshape(-1, SW), "freq", axis=0, tiled=True)
    response = lax.all_gather(response, "panel", axis=0, tiled=True)
    response = response.reshape(-1, steps * owners, each, SW)
    return convolve(shot_gathers, response, owners)


def transform_tables(freq_total, time_total):
    bins = jnp.arange(freq_total, dtype=jnp.int32) + 1
    times = jnp.arange(time_total, dtype=jnp.int32)
    phase = bins[:, None] * times[None, :] % time_total
    angle = phase.astype(jnp.float32) * (2.0 * math.pi / time_total)
    scale = 1.0 / math.sqrt(time_total)
    forward = jnp.stack([jnp.cos(angle) * scale, -jnp.sin(angle) * scale], axis=1).astype(
        jnp.bfloat16
    )
    inverse = jnp.stack([jnp.cos(angle), -jnp.sin(angle)], axis=1).astype(jnp.bfloat16)
    return (forward, inverse)


def frequency_body(shot_gathers, aperture_blocks, taper_index):
    time_local, rows_local, points_total = shot_gathers.shape
    owners = lax.axis_size("freq")
    slot_count = 2 * F_DEV
    time_total = time_local * owners
    freq_total = F_DEV * owners
    owner_index = lax.axis_index("freq")
    panel_index = lax.axis_index("panel")
    owner_range = jnp.arange(owners, dtype=jnp.int32)
    freq_range = jnp.arange(freq_total, dtype=jnp.int32)
    assignment = freq_range.reshape(owners, F_DEV)
    forward, inverse = transform_tables(freq_total, time_total)
    selector = (assignment.reshape(-1)[:, None] == freq_range[None, :]).astype(jnp.bfloat16)
    picked_forward = jnp.dot(
        selector, forward.reshape(freq_total, 2 * time_total), preferred_element_type=jnp.float32
    ).astype(jnp.bfloat16)
    forward_rows = (
        picked_forward.reshape(owners, F_DEV, 2, time_total)
        .transpose(1, 2, 0, 3)
        .reshape(slot_count, owners, time_total)
    )
    picked_inverse = jnp.dot(
        selector, inverse.reshape(freq_total, 2 * time_total), preferred_element_type=jnp.float32
    ).astype(jnp.bfloat16)
    inverse_rows = picked_inverse.reshape(owners * slot_count, owners, time_local)
    trace_width = rows_local * points_total // owners
    outgoing_time = shot_gathers.reshape(time_local, owners, trace_width)
    series = lax.all_to_all(outgoing_time, "freq", split_axis=1, concat_axis=0, tiled=True)[:, 0, :]
    spectra = jnp.einsum(
        "qot,tw->qow", forward_rows, series, preferred_element_type=jnp.float32
    ).astype(jnp.bfloat16)
    own_spectra = lax.all_to_all(spectra, "freq", split_axis=1, concat_axis=1, tiled=True)
    own_spectra = own_spectra.reshape(F_DEV, 2, rows_local, points_total)
    mine = owner_range[:, None] == owner_index
    my_freqs = jnp.sum(jnp.where(mine, assignment, jnp.zeros_like(assignment)), axis=0)
    matches = my_freqs[:, None] == freq_range[None, :]
    my_aperture = jnp.sum(jnp.where(matches, aperture_blocks[None, :], 0), axis=1)
    my_taper = jnp.sum(jnp.where(matches, taper_index[None, :], 0), axis=1)
    local_points = panel_index * rows_local + jnp.arange(rows_local, dtype=jnp.int32)
    weights = taper_weights(my_aperture[:, None], my_taper[:, None], local_points[None, :])
    tapered = (weights[:, None, :, None] * own_spectra[:, :, :, :SW].astype(jnp.float32)).astype(
        jnp.bfloat16
    )
    piece = lax.all_gather(tapered, "panel", axis=2, tiled=True)
    updated_list = []
    for slot_index in range(F_DEV):
        left_block = own_spectra[slot_index]
        stacked_left = jnp.concatenate([left_block[0], left_block[1]], axis=1)
        real_side = jnp.concatenate([piece[slot_index, 0], -piece[slot_index, 1]], axis=0)
        imag_side = jnp.concatenate([piece[slot_index, 1], piece[slot_index, 0]], axis=0)
        stacked_right = jnp.stack([real_side, imag_side], axis=0)
        updated = jnp.einsum(
            "rk,cks->crs", stacked_left, stacked_right, preferred_element_type=jnp.float32
        )
        updated_list.append(updated)
    summed = jnp.stack(updated_list, axis=0)
    multiples = (summed * (-1.0 / math.sqrt(points_total))).astype(jnp.bfloat16)
    output_width = rows_local * SW // owners
    outgoing_freq = multiples.reshape(slot_count, owners, output_width)
    output_scale = 1.0 / math.sqrt(freq_total)
    values = lax.all_to_all(outgoing_freq, "freq", split_axis=1, concat_axis=0, tiled=True)[:, 0, :]
    traces = (
        jnp.einsum("qgt,qw->tgw", inverse_rows, values, preferred_element_type=jnp.float32)
        * output_scale
    )
    result = lax.all_to_all(
        traces.astype(jnp.bfloat16), "freq", split_axis=1, concat_axis=1, tiled=True
    )
    return result.reshape(time_local, rows_local, SW)


def solution(mesh):
    return jax.shard_map(
        body,
        mesh=mesh,
        in_specs=(P("freq", "panel", None), P(), P()),
        out_specs=P("freq", "panel", None),
        check_vma=False,
    )
```
